32 devices in a mesh: groups: 2 (over x), resp: 16 (over z, y, core).
Axes of the slice: x: 2, y: 2, z: 4, core: 2. Of those that a mesh axis runs over, the one named last changes fastest.
Arguments:
- queries: bfloat16 [32, 128, 2048], P(('groups', 'resp')), parts along dimension 0, may hold values from -6 to 6
- resp_keys: bfloat16 [32, 128, 512], P(('groups', 'resp')), parts along dimension 0, may hold values from -6 to 6
- resp_values: bfloat16 [32, 128, 512], P(('groups', 'resp')), parts along dimension 0, may hold values from -6 to 6
- out_grad: bfloat16 [32, 128, 2048], P(('groups', 'resp')), parts along dimension 0, may hold values from -6 to 6
- resp_lengths: int32 [32], P(('groups', 'resp')), parts along dimension 0, may hold values from 1 to 128, 1280 in all
- prompt_keys: bfloat16 [1024, 512], P(('groups', 'resp')), parts along dimension 0, may hold values from -6 to 6
- prompt_values: bfloat16 [1024, 512], P(('groups', 'resp')), parts along dimension 0, may hold values from -6 to 6
- prompt_length: int32 [2], P('groups'), parts along dimension 0, may hold values from 256 to 512
Outputs:
- attn_out: bfloat16 [32, 128, 2048], P(('groups', 'resp')), parts along dimension 0
- query_grad: bfloat16 [32, 128, 2048], P(('groups', 'resp')), parts along dimension 0
- key_grad: bfloat16 [32, 128, 512], P(('groups', 'resp')), parts along dimension 0
- value_grad: bfloat16 [32, 128, 512], P(('groups', 'resp')), parts along dimension 0
- prompt_key_grad: float32 [1024, 512], P(('groups', 'resp')), parts along dimension 0
- prompt_value_grad: float32 [1024, 512], P(('groups', 'resp')), parts along dimension 0
The draws below stay inside these ranges and needn't reach their ends.
There are 2 independent parts, one for each index of `groups`. The reference program is written for one: setup_inputs(seed, part) draws one part's arguments, and reference() takes and returns one part's arrays. A program takes and returns all parts, laid end to end along the dimension named above; each array names one. Nothing has to cross between parts.
All inputs are finite; a program needn't handle non-finite values. No bound on the sum of `resp_lengths` on one device may be relied on, other than what follows from the above.
Results may differ from the reference program's by a relative error of at most 0.0095.
Values may be sent and summed in bfloat16 or wider, within the bound.
A program may use at most 64 MiB of HBM per device.

```python
import math
import jax
import jax.numpy as jnp
import numpy as np
from jax import lax

HEADS = 16
KV_HEADS = 4
HEAD_DIM = 128
RESP_LEN = 128
NRESP = 16
PROMPT = 512


def draw_queries(key, part):
    key = jax.random.fold_in(key, 11)
    first, second = jax.random.split(key)
    row_scales = jnp.exp(jax.random.uniform(second, (NRESP, RESP_LEN, 1, 1), minval=math.log(1.0), maxval=math.log(3.0)))
    base = jax.random.normal(first, (NRESP, RESP_LEN, HEADS, HEAD_DIM))
    values = jnp.clip(base * row_scales, -5.9, 5.9)
    return values.reshape(NRESP, RESP_LEN, HEADS * HEAD_DIM).astype(jnp.bfloat16)


def draw_prompt_keys(key, part):
    key = jax.random.fold_in(key, 12)
    first, second = jax.random.split(key)
    row_scales = jnp.exp(jax.random.uniform(second, (PROMPT, 1, 1), minval=math.log(1.5), maxval=math.log(3.0)))
    base = jax.random.normal(first, (PROMPT, KV_HEADS, HEAD_DIM))
    values = jnp.clip(base * row_scales, -5.9, 5.9)
    return values.reshape(PROMPT, KV_HEADS * HEAD_DIM).astype(jnp.bfloat16)


def steps_of(own_key, shape, pieces, smallest, high):
    def one(position, parts):
        draws = jax.random.uniform(jax.random.fold_in(jax.random.fold_in(own_key, 6), position), (parts,), jnp.float32, smallest / len(pieces), high / len(pieces))
        return jnp.repeat(jnp.exp(draws), shape[position] // parts).reshape((-1,) + (1,) * (len(shape) - position - 1))

    gain = one(*pieces[0])
    for cut in pieces[1:]:
        gain = gain * one(*cut)
    return gain


def split_up(number_of, total, limit, lean):
    portions = [(1 << 20) // math.isqrt(rank ** lean) + 1 for rank in range(2, number_of + 1)]
    surplus, given = total - limit - (number_of - 1), [1] * (number_of - 1)
    while surplus > 0:
        candidates = [i for i in range(number_of - 1) if given[i] < limit]
        whole, left = sum([portions[i] for i in candidates]), surplus
        for i in candidates:
            addition = min(limit - given[i], max(1, left * portions[i] // whole), surplus)
            given[i] = given[i] + addition
            surplus = surplus - addition
    return np.array([limit] + given)


def ragged_sizes(rng, count, total, most, skew):
    if count == 2:
        one = jax.random.randint(rng, (), max(1, total - most), min(most, total - 1) + 1)
        return jnp.stack([one, total - one])
    sizes = jnp.asarray(split_up(count, total, most, skew), jnp.int32)
    twos = (count - 1) // 2
    donor, sink = sizes[1:1 + 2 * twos:2], sizes[2:2 + 2 * twos:2]
    margin = jnp.minimum(donor - 1, most - sink)
    moved = jax.random.randint(jax.random.fold_in(rng, 1), (twos,), 0, 1 << 20) % (margin + 1)
    sizes = sizes.at[1:1 + 2 * twos:2].set(donor - moved).at[2:2 + 2 * twos:2].set(sink + moved)
    return sizes[jax.random.permutation(jax.random.fold_in(rng, 2), count)]


def normal_values(rng, extent, width, most, cuts=(), held_as=jnp.bfloat16):
    array = jax.random.normal(rng, extent, jnp.float32) * width
    if len(cuts) > 0:
        array = steps_of(rng, extent, cuts, -0.22, 0.18) * array
    return jnp.clip(array, min=-most, max=most).astype(held_as)


def setup_inputs(seed: int = 0, part: int = 0) -> dict:
    seeds = jax.random.split(jax.random.key(seed), 9)
    part_splits = jax.random.split(jax.random.fold_in(seeds[8], part), 9)
    return {
        "queries": draw_queries(jax.random.fold_in(jax.random.fold_in(seeds[8], part), 71), part),
        "resp_keys": normal_values(part_splits[1], (NRESP, RESP_LEN, KV_HEADS * HEAD_DIM), 1.0, 6.0, ((0, 16),)),
        "resp_values": normal_values(part_splits[2], (NRESP, RESP_LEN, KV_HEADS * HEAD_DIM), 1.0, 6.0, ((0, 16),)),
        "out_grad": normal_values(part_splits[3], (NRESP, RESP_LEN, HEADS * HEAD_DIM), 1.0, 6.0, ((0, 16),)),
        "resp_lengths": ragged_sizes(part_splits[4], NRESP, NRESP * RESP_LEN * 5 // 8, RESP_LEN, 1).astype(jnp.int32),
        "prompt_keys": draw_prompt_keys(jax.random.fold_in(jax.random.fold_in(seeds[8], part), 71), part),
        "prompt_values": normal_values(part_splits[6], (PROMPT, KV_HEADS * HEAD_DIM), 1.0, 6.0, ((0, 16),)),
        "prompt_length": jax.random.randint(part_splits[7], (1,), PROMPT // 2, PROMPT + 1).astype(jnp.int32),
    }


def product(form, left, right):
    return jnp.einsum(form, left.astype(jnp.float32), right.astype(jnp.float32), precision=lax.Precision.HIGHEST)


def head_core(query_head, key_self, value_self, grad_head, key_prompt, value_prompt, live_prompt, causal, row_mask):
    scaling = query_head.shape[-1] ** -0.5
    prompt_rows = key_prompt.shape[0]
    score_prompt = product("rigd,pd->rgip", query_head, key_prompt) * scaling
    score_prompt = jnp.where(live_prompt[None, None, None, :], score_prompt, -jnp.inf)
    score_self = product("rigd,rjd->rgij", query_head, key_self) * scaling
    score_self = jnp.where(causal[None, None], score_self, -jnp.inf)
    scores = jnp.concatenate([score_prompt, score_self], -1)
    maxima = jnp.max(scores, -1, keepdims=True)
    exponent = jnp.exp(scores - maxima)
    weights = exponent / jnp.sum(exponent, -1, keepdims=True)
    weights_low = weights.astype(jnp.bfloat16)
    attended = product("rgip,pd->rigd", weights_low[..., :prompt_rows], value_prompt)
    attended = attended + product("rgij,rjd->rigd", weights_low[..., prompt_rows:], value_self)
    attended_low = (attended * row_mask[:, :, None, None]).astype(jnp.bfloat16)
    row_dot = jnp.sum(grad_head.astype(jnp.float32) * attended_low.astype(jnp.float32), -1)
    grad_weights = jnp.concatenate([product("rigd,pd->rgip", grad_head, value_prompt), product("rigd,rjd->rgij", grad_head, value_self)], -1)
    score_grad = (weights * (grad_weights - jnp.transpose(row_dot, (0, 2, 1))[..., None])).astype(jnp.bfloat16)
    grad_prompt = score_grad[..., :prompt_rows]
    grad_self = score_grad[..., prompt_rows:]
    query_grad = ((product("rgip,pd->rigd", grad_prompt, key_prompt) + product("rgij,rjd->rigd", grad_self, key_self)) * scaling).astype(jnp.bfloat16)
    selfkey_grad = (product("rgij,rigd->rjd", grad_self, query_head) * scaling).astype(jnp.bfloat16)
    selfval_grad = product("rgij,rigd->rjd", weights_low[..., prompt_rows:], grad_head).astype(jnp.bfloat16)
    promptk_grad = product("rgip,rigd->pd", grad_prompt, query_head) * scaling
    promptv_grad = product("rgip,rigd->pd", weights_low[..., :prompt_rows], grad_head)
    return attended_low, query_grad, selfkey_grad, selfval_grad, promptk_grad, promptv_grad


def reference(queries, resp_keys, resp_values, out_grad, resp_lengths, prompt_keys, prompt_values, prompt_length):
    group_size = HEADS // KV_HEADS
    live_prompt = jnp.arange(PROMPT) < prompt_length[0]
    positions = jnp.arange(RESP_LEN)
    causal = positions[None, :] <= positions[:, None]
    pkey_heads = prompt_keys.reshape(PROMPT, KV_HEADS, HEAD_DIM)
    pval_heads = prompt_values.reshape(PROMPT, KV_HEADS, HEAD_DIM)

    def respond(totals, inputs):
        query_row, key_row, value_row, grad_row, resp_len = inputs
        row_mask = (positions < resp_len)[None, :]
        masked = grad_row * row_mask[0][:, None].astype(grad_row.dtype)
        query_five = query_row.reshape(1, RESP_LEN, KV_HEADS, group_size, HEAD_DIM)
        grad_five = masked.reshape(1, RESP_LEN, KV_HEADS, group_size, HEAD_DIM)
        key_four = key_row.reshape(1, RESP_LEN, KV_HEADS, HEAD_DIM)
        value_four = value_row.reshape(1, RESP_LEN, KV_HEADS, HEAD_DIM)
        outcomes = [head_core(query_five[:, :, head_index], key_four[:, :, head_index], value_four[:, :, head_index], grad_five[:, :, head_index], pkey_heads[:, head_index], pval_heads[:, head_index], live_prompt, causal, row_mask) for head_index in range(KV_HEADS)]
        attended = jnp.stack([outcome[0] for outcome in outcomes], 2).reshape(RESP_LEN, HEADS * HEAD_DIM)
        query_grad = jnp.stack([outcome[1] for outcome in outcomes], 2).reshape(RESP_LEN, HEADS * HEAD_DIM)
        selfkey_grad = jnp.stack([outcome[2] for outcome in outcomes], 2).reshape(RESP_LEN, KV_HEADS * HEAD_DIM)
        selfval_grad = jnp.stack([outcome[3] for outcome in outcomes], 2).reshape(RESP_LEN, KV_HEADS * HEAD_DIM)
        promptk_grad = jnp.stack([outcome[4] for outcome in outcomes], 1).reshape(PROMPT, KV_HEADS * HEAD_DIM)
        promptv_grad = jnp.stack([outcome[5] for outcome in outcomes], 1).reshape(PROMPT, KV_HEADS * HEAD_DIM)
        return (totals[0] + promptk_grad, totals[1] + promptv_grad), (attended, query_grad, selfkey_grad, selfval_grad)

    empty_sum = jnp.zeros((PROMPT, KV_HEADS * HEAD_DIM), jnp.float32)
    totals, per_resp = lax.scan(respond, (empty_sum, empty_sum), (queries, resp_keys, resp_values, out_grad, resp_lengths))
    return per_resp[0], per_resp[1], per_resp[2], per_resp[3], totals[0], totals[1]
```

```python
import functools
import math

import jax
import jax.numpy as jnp
from jax import lax
from jax.experimental import pallas as pl
from jax.experimental.pallas import tpu as pltpu
from jax.sharding import PartitionSpec as P

HEADS = 16
KV_HEADS = 4
HEAD_DIM = 128
GROUP = HEADS // KV_HEADS
CORES = 2
PAIRS = 2
F32 = jnp.float32
BF16 = jnp.bfloat16


def nt(left, right):
    return lax.dot_general(left, right, (((1,), (1,)), ((), ())), preferred_element_type=F32)


def tn(left, right):
    return lax.dot_general(left, right, (((0,), (0,)), ((), ())), preferred_element_type=F32)


def nn(left, right):
    return lax.dot_general(left, right, (((1,), (0,)), ((), ())), preferred_element_type=F32)


def kernel(
    far,
    q_hbm, rk_ref, rv_ref, og_hbm, len_ref, pk_ref, pv_ref, plen_ref,
    o_hbm, dq_hbm, dk_ref, dv_ref, dpk_ref, dpv_ref,
    q, og, ob, dqb, held, part, from_core, core_sum, from_pair, pair_sum, from_far, bias,
    load_sem, store_sem,
    s1, r1, s2, r2, s3, r3, sa, ra, sb, rb, sc, rc,
):
    me = lax.axis_index("resp")
    c = lax.rem(me, CORES)
    y = lax.rem(lax.div(me, CORES), PAIRS)
    z = lax.div(me, CORES * PAIRS)
    rows = pk_ref.shape[0]
    prompt = rows * far * PAIRS * CORES
    length = q_hbm.shape[1]
    wide = GROUP * length
    scaling = HEAD_DIM ** -0.5

    def device(zz, yy, cc):
        return {"resp": (zz * PAIRS + yy) * CORES + cc}

    def remote(src, dst, send, recv, target):
        return pltpu.make_async_remote_copy(
            src_ref=src, dst_ref=dst, send_sem=send, recv_sem=recv,
            device_id=target, device_id_type=pl.DeviceIdType.MESH,
        )

    def ahead(d):
        return lax.rem(z + d, far)

    def behind(d):
        return lax.rem(z + (far - d), far)

    pair_dev = device(z, 1 - y, c)
    core_dev = device(z, y, 1 - c)

    q_load = pltpu.make_async_copy(q_hbm.at[0], q, load_sem.at[0])
    og_load = pltpu.make_async_copy(og_hbm.at[0], og, load_sem.at[1])
    q_load.start()
    og_load.start()

    barrier = pltpu.get_barrier_semaphore()
    for d in range(1, far):
        pl.semaphore_signal(barrier, inc=1, device_id=device(ahead(d), y, c),
                            device_id_type=pl.DeviceIdType.MESH)
    pl.semaphore_signal(barrier, inc=1, device_id=pair_dev, device_id_type=pl.DeviceIdType.MESH)
    pl.semaphore_signal(barrier, inc=1, device_id=core_dev, device_id_type=pl.DeviceIdType.MESH)

    for h in range(KV_HEADS):
        lanes = slice(h * HEAD_DIM, (h + 1) * HEAD_DIM)
        held[h, c, y, z, :, :HEAD_DIM] = pk_ref[:, lanes]
        held[h, c, y, z, :, HEAD_DIM:] = pv_ref[:, lanes]

    pl.semaphore_wait(barrier, far + 1)

    def gather_far(h, d, slot):
        return remote(held.at[h, c, y, slot], held.at[h, c, y, slot],
                      s1.at[h, d - 1], r1.at[h, d - 1], device(ahead(d), y, c))

    def gather_pair(h, yy):
        return remote(held.at[h, c, yy], held.at[h, c, yy], s2.at[h], r2.at[h], pair_dev)

    def gather_core(h, cc):
        return remote(held.at[h, cc], held.at[h, cc], s3.at[h], r3.at[h], core_dev)

    def pass_pair(h):
        for d in range(1, far):
            gather_far(h, d, behind(d)).wait_recv()
        gather_pair(h, y).start()

    def pass_core(h):
        gather_pair(h, 1 - y).wait_recv()
        gather_core(h, c).start()

    def reduce_core(h):
        return remote(part.at[h, 1 - c], from_core.at[h], sa.at[h], ra.at[h], core_dev)

    def reduce_pair(h):
        return remote(core_sum.at[h, 1 - y], from_pair.at[h], sb.at[h], rb.at[h], pair_dev)

    def reduce_far(h, d):
        return remote(pair_sum.at[h, ahead(d)], from_far.at[h, d - 1],
                      sc.at[h, d - 1], rc.at[h, d - 1], device(ahead(d), y, c))

    def add_core(h):
        reduce_core(h).wait_recv()
        core_sum[h] = (part[h, c].astype(F32) + from_core[h].astype(F32)).astype(BF16)
        reduce_pair(h).start()

    def add_pair(h):
        reduce_pair(h).wait_recv()
        pair_sum[h] = (core_sum[h, y].astype(F32) + from_pair[h].astype(F32)).astype(BF16)
        for d in range(1, far):
            reduce_far(h, d).start()

    def add_far(h):
        total = pair_sum[h, z].astype(F32)
        for d in range(1, far):
            reduce_far(h, d).wait_recv()
            total = total + from_far[h, d - 1].astype(F32)
        lanes = slice(h * HEAD_DIM, (h + 1) * HEAD_DIM)
        dpk_ref[:, lanes] = total[:, :HEAD_DIM] * scaling
        dpv_ref[:, lanes] = total[:, HEAD_DIM:]

    for h in range(KV_HEADS):
        for d in range(1, far):
            gather_far(h, d, z).start()

    index = lax.broadcasted_iota(jnp.int32, (prompt, length), 0)
    block = lax.div(index, rows)
    owner = (
        lax.rem(block, far) * (PAIRS * CORES)
        + lax.rem(lax.div(block, far), PAIRS) * CORES
        + lax.div(block, far * PAIRS)
    )
    position = owner * rows + lax.rem(index, rows)
    bias[...] = jnp.where(position < plen_ref[0], 0.0, -jnp.inf)
    below = lax.broadcasted_iota(jnp.int32, (length, length), 0)
    after = lax.broadcasted_iota(jnp.int32, (length, length), 1)
    causal = jnp.where(below <= after, 0.0, -jnp.inf)
    live = below < len_ref[0]

    def out_store(h):
        lanes = pl.ds(h * GROUP * HEAD_DIM, GROUP * HEAD_DIM)
        return pltpu.make_async_copy(ob.at[:, lanes], o_hbm.at[0, :, lanes], store_sem.at[0, h])

    def dq_store(h):
        lanes = pl.ds(h * GROUP * HEAD_DIM, GROUP * HEAD_DIM)
        return pltpu.make_async_copy(dqb.at[:, lanes], dq_hbm.at[0, :, lanes], store_sem.at[1, h])

    def head_lanes(h, i):
        return slice((h * GROUP + i) * HEAD_DIM, (h * GROUP + i + 1) * HEAD_DIM)

    def compute(h):
        lanes = slice(h * HEAD_DIM, (h + 1) * HEAD_DIM)
        key_self, value_self = rk_ref[0, :, lanes], rv_ref[0, :, lanes]
        query = jnp.concatenate([q[:, head_lanes(h, i)] for i in range(GROUP)], 0)
        grad = jnp.concatenate(
            [jnp.where(live, og[:, head_lanes(h, i)], jnp.zeros((), BF16)) for i in range(GROUP)], 0
        )
        both = held[h].reshape(prompt, 2 * HEAD_DIM)
        key, value = both[:, :HEAD_DIM], both[:, HEAD_DIM:]
        masks = jnp.concatenate([bias[...]] * GROUP, 1)
        causals = jnp.concatenate([causal] * GROUP, 1)
        score_p = nt(key, query) + masks
        score_s = nt(key_self, query) + causals
        top = jnp.maximum(
            jnp.max(score_p, 0, keepdims=True), jnp.max(score_s, 0, keepdims=True)
        )
        factor = scaling * math.log2(math.e)
        exp_p = jnp.exp2((score_p - top) * factor)
        exp_s = jnp.exp2((score_s - top) * factor)
        inverse = 1.0 / (jnp.sum(exp_p, 0, keepdims=True) + jnp.sum(exp_s, 0, keepdims=True))
        weight_p, weight_s = exp_p * inverse, exp_s * inverse
        low_p, low_s = weight_p.astype(BF16), weight_s.astype(BF16)
        part_v = nn(low_p, grad)
        gw_p, gw_s = nt(value, grad), nt(value_self, grad)
        dot = jnp.sum(weight_p * gw_p, 0, keepdims=True) + jnp.sum(weight_s * gw_s, 0, keepdims=True)
        sg_p = (weight_p * (gw_p - dot)).astype(BF16)
        sg_s = (weight_s * (gw_s - dot)).astype(BF16)
        part_k = nn(sg_p, query)
        shape = (CORES, PAIRS, far, rows, HEAD_DIM)
        part[h, :, :, :, :, :HEAD_DIM] = part_k.astype(BF16).reshape(shape)
        part[h, :, :, :, :, HEAD_DIM:] = part_v.astype(BF16).reshape(shape)
        reduce_core(h).start()
        out_t = tn(value, low_p) + tn(value_self, low_s)
        dq_t = (tn(key, sg_p) + tn(key_self, sg_s)) * scaling
        for i in range(GROUP):
            cut = slice(i * length, (i + 1) * length)
            ob[:, head_lanes(h, i)] = jnp.where(live, out_t[:, cut].T, 0.0).astype(BF16)
            dqb[:, head_lanes(h, i)] = dq_t[:, cut].T.astype(BF16)
        out_store(h).start()
        dq_store(h).start()
        dk_ref[0, :, lanes] = (nn(sg_s, query) * scaling).astype(BF16)
        dv_ref[0, :, lanes] = nn(low_s, grad).astype(BF16)

    last = KV_HEADS - 1
    pass_pair(0)
    pass_pair(1)
    pass_core(0)
    pass_pair(2)
    pass_core(1)
    pass_pair(3)
    q_load.wait()
    og_load.wait()
    for h in range(KV_HEADS):
        if h == 1:
            pass_core(2)
            pass_core(3)
        gather_core(h, 1 - c).wait_recv()
        compute(h)
        if h >= 1:
            add_core(h - 1)
        if h >= 2:
            add_pair(h - 2)
    add_core(last)
    add_pair(last - 1)
    for h in range(last):
        add_far(h)
    add_pair(last)
    for h in range(KV_HEADS):
        out_store(h).wait()
        dq_store(h).wait()
        for d in range(1, far):
            gather_far(h, d, z).wait_send()
        gather_pair(h, y).wait_send()
        gather_core(h, c).wait_send()
        reduce_core(h).wait_send()
        reduce_pair(h).wait_send()
    add_far(last)
    for h in range(KV_HEADS):
        for d in range(1, far):
            reduce_far(h, d).wait_send()


def on_device(far, queries, resp_keys, resp_values, out_grad, resp_lengths, prompt_keys, prompt_values, prompt_length):
    length, width = queries.shape[1:]
    rows, kv_width = prompt_keys.shape
    prompt = rows * far * PAIRS * CORES
    any_spec = pl.BlockSpec(memory_space=pl.ANY)
    vmem = pl.BlockSpec(memory_space=pltpu.VMEM)
    smem = pl.BlockSpec(memory_space=pltpu.SMEM)
    both = 2 * HEAD_DIM
    dma = pltpu.SemaphoreType.DMA
    return pl.pallas_call(
        functools.partial(kernel, far),
        out_shape=(
            jax.ShapeDtypeStruct(queries.shape, BF16),
            jax.ShapeDtypeStruct(queries.shape, BF16),
            jax.ShapeDtypeStruct(resp_keys.shape, BF16),
            jax.ShapeDtypeStruct(resp_keys.shape, BF16),
            jax.ShapeDtypeStruct(prompt_keys.shape, F32),
            jax.ShapeDtypeStruct(prompt_keys.shape, F32),
        ),
        in_specs=[any_spec, vmem, vmem, any_spec, smem, vmem, vmem, smem],
        out_specs=(any_spec, any_spec, vmem, vmem, vmem, vmem),
        scratch_shapes=[
            pltpu.VMEM((length, width), BF16),
            pltpu.VMEM((length, width), BF16),
            pltpu.VMEM((length, width), BF16),
            pltpu.VMEM((length, width), BF16),
            pltpu.VMEM((KV_HEADS, CORES, PAIRS, far, rows, both), BF16),
            pltpu.VMEM((KV_HEADS, CORES, PAIRS, far, rows, both), BF16),
            pltpu.VMEM((KV_HEADS, PAIRS, far, rows, both), BF16),
            pltpu.VMEM((KV_HEADS, PAIRS, far, rows, both), BF16),
            pltpu.VMEM((KV_HEADS, far, rows, both), BF16),
            pltpu.VMEM((KV_HEADS, far, rows, both), BF16),
            pltpu.VMEM((KV_HEADS, far - 1, rows, both), BF16),
            pltpu.VMEM((prompt, length), F32),
            dma((2,)),
            dma((2, KV_HEADS)),
            dma((KV_HEADS, far - 1)), dma((KV_HEADS, far - 1)),
            dma((KV_HEADS,)), dma((KV_HEADS,)),
            dma((KV_HEADS,)), dma((KV_HEADS,)),
            dma((KV_HEADS,)), dma((KV_HEADS,)),
            dma((KV_HEADS,)), dma((KV_HEADS,)),
            dma((KV_HEADS, far - 1)), dma((KV_HEADS, far - 1)),
        ],
        compiler_params=pltpu.CompilerParams(
            collective_id=0, has_side_effects=True, vmem_limit_bytes=60 * 1024 * 1024
        ),
    )(queries, resp_keys, resp_values, out_grad, resp_lengths, prompt_keys, prompt_values, prompt_length)


def solution(mesh):
    far = mesh.shape["resp"] // (CORES * PAIRS)
    shard = P(("groups", "resp"), None, None)
    flat = P(("groups", "resp"), None)
    return jax.shard_map(
        functools.partial(on_device, far),
        mesh=mesh,
        in_specs=(shard, shard, shard, shard, P(("groups", "resp")), flat, flat, P("groups")),
        out_specs=(shard, shard, shard, shard, flat, flat),
        check_vma=False,
    )
```

```python
import functools
import math

import jax
import jax.numpy as jnp
from jax import lax
from jax.experimental import pallas as pl
from jax.experimental.pallas import tpu as pltpu
from jax.sharding import PartitionSpec as P

HEADS = 16
KV_HEADS = 4
HEAD_DIM = 128
GROUP = HEADS // KV_HEADS
CORES = 2
PAIRS = 2
F32 = jnp.float32
BF16 = jnp.bfloat16


def nt(left, right):
    return lax.dot_general(left, right, (((1,), (1,)), ((), ())), preferred_element_type=F32)


def tn(left, right):
    return lax.dot_general(left, right, (((0,), (0,)), ((), ())), preferred_element_type=F32)


def nn(left, right):
    return lax.dot_general(left, right, (((1,), (0,)), ((), ())), preferred_element_type=F32)


def kernel(
    far,
    q_hbm, rk_hbm, rv_hbm, og_hbm, len_ref, pk_hbm, pv_hbm, plen_ref,
    o_ref, dq_ref, dk_ref, dv_ref, dpk_ref, dpv_ref,
    q, og, rk, rv, pk, pv, held, part, from_core, core_sum, from_pair, pair_sum, from_far, bias,
    load_sem,
    s1, r1, s2, r2, s3, r3, sa, ra, sb, rb, sc, rc,
):
    me = lax.axis_index("resp")
    c = lax.rem(me, CORES)
    y = lax.rem(lax.div(me, CORES), PAIRS)
    z = lax.div(me, CORES * PAIRS)
    rows = pk_hbm.shape[0]
    prompt = rows * far * PAIRS * CORES
    length = q_hbm.shape[1]
    wide = GROUP * length
    scaling = HEAD_DIM ** -0.5

    def device(zz, yy, cc):
        return {"resp": (zz * PAIRS + yy) * CORES + cc}

    def remote(src, dst, send, recv, target):
        return pltpu.make_async_remote_copy(
            src_ref=src, dst_ref=dst, send_sem=send, recv_sem=recv,
            device_id=target, device_id_type=pl.DeviceIdType.MESH,
        )

    def ahead(d):
        return lax.rem(z + d, far)

    def behind(d):
        return lax.rem(z + (far - d), far)

    pair_dev = device(z, 1 - y, c)
    core_dev = device(z, y, 1 - c)

    loads = [
        pltpu.make_async_copy(src, dst, load_sem.at[i])
        for i, (src, dst) in enumerate((
            (pk_hbm, pk), (pv_hbm, pv), (rk_hbm.at[0], rk), (rv_hbm.at[0], rv),
            (q_hbm.at[0], q), (og_hbm.at[0], og),
        ))
    ]
    for load in loads:
        load.start()

    barrier = pltpu.get_barrier_semaphore()
    for d in range(1, far):
        pl.semaphore_signal(barrier, inc=1, device_id=device(ahead(d), y, c),
                            device_id_type=pl.DeviceIdType.MESH)
    pl.semaphore_signal(barrier, inc=1, device_id=pair_dev, device_id_type=pl.DeviceIdType.MESH)
    pl.semaphore_signal(barrier, inc=1, device_id=core_dev, device_id_type=pl.DeviceIdType.MESH)

    loads[0].wait()
    loads[1].wait()
    for h in range(KV_HEADS):
        lanes = slice(h * HEAD_DIM, (h + 1) * HEAD_DIM)
        held[h, c, y, z, :, :HEAD_DIM] = pk[:, lanes]
        held[h, c, y, z, :, HEAD_DIM:] = pv[:, lanes]

    pl.semaphore_wait(barrier, far + 1)

    def gather_far(h, d, slot):
        return remote(held.at[h, c, y, slot], held.at[h, c, y, slot],
                      s1.at[h, d - 1], r1.at[h, d - 1], device(ahead(d), y, c))

    def gather_pair(h, d, yy):
        slot = behind(d)
        return remote(held.at[h, c, yy, slot], held.at[h, c, yy, slot],
                      s2.at[h, d], r2.at[h, d], pair_dev)

    def gather_core(h, cc):
        return remote(held.at[h, cc], held.at[h, cc], s3.at[h], r3.at[h], core_dev)

    def start_far(h):
        for d in range(1, far):
            gather_far(h, d, z).start()
        gather_pair(h, 0, y).start()

    def pass_pair(h):
        for d in range(1, far):
            gather_far(h, d, behind(d)).wait_recv()
            gather_pair(h, d, y).start()

    def pass_core(h):
        for d in range(far):
            gather_pair(h, d, 1 - y).wait_recv()
        gather_core(h, c).start()

    steps = [*range(1, far), 0]

    def reduce_core(h):
        return remote(part.at[h, 1 - c], from_core.at[h], sa.at[h], ra.at[h], core_dev)

    def reduce_pair(h, d):
        slot = ahead(d)
        return remote(core_sum.at[h, slot], from_pair.at[h, slot], sb.at[h, d], rb.at[h, d], pair_dev)

    def reduce_far(h, d):
        return remote(pair_sum.at[h, d - 1], from_far.at[h, d - 1],
                      sc.at[h, d - 1], rc.at[h, d - 1], device(ahead(d), y, c))

    def add_core(h):
        reduce_core(h).wait_recv()
        for d in steps:
            slot = ahead(d)
            core_sum[h, slot] = (
                part[h, c, 1 - y, slot].astype(F32) + from_core[h, 1 - y, slot].astype(F32)
            ).astype(BF16)
            reduce_pair(h, d).start()

    def own_sum(h, d):
        slot = ahead(d)
        reduce_pair(h, d).wait_recv()
        return (
            part[h, c, y, slot].astype(F32)
            + from_core[h, y, slot].astype(F32)
            + from_pair[h, slot].astype(F32)
        )

    def add_pair(h):
        for d in range(1, far):
            pair_sum[h, d - 1] = own_sum(h, d).astype(BF16)
            reduce_far(h, d).start()

    def add_far(h):
        total = own_sum(h, 0)
        for d in range(1, far):
            reduce_far(h, d).wait_recv()
            total = total + from_far[h, d - 1].astype(F32)
        lanes = slice(h * HEAD_DIM, (h + 1) * HEAD_DIM)
        dpk_ref[:, lanes] = total[:, :HEAD_DIM] * scaling
        dpv_ref[:, lanes] = total[:, HEAD_DIM:]

    start_far(0)
    start_far(1)

    index = lax.broadcasted_iota(jnp.int32, (prompt, length), 0)
    block = lax.div(index, rows)
    owner = (
        lax.rem(block, far) * (PAIRS * CORES)
        + lax.rem(lax.div(block, far), PAIRS) * CORES
        + lax.div(block, far * PAIRS)
    )
    position = owner * rows + lax.rem(index, rows)
    bias[...] = jnp.where(position < plen_ref[0], 0.0, -jnp.inf)
    below = lax.broadcasted_iota(jnp.int32, (length, length), 0)
    after = lax.broadcasted_iota(jnp.int32, (length, length), 1)
    causal = jnp.where(below <= after, 0.0, -jnp.inf)
    live = below < len_ref[0]

    def head_lanes(h, i):
        return slice((h * GROUP + i) * HEAD_DIM, (h * GROUP + i + 1) * HEAD_DIM)

    def compute(h, between):
        lanes = slice(h * HEAD_DIM, (h + 1) * HEAD_DIM)
        key_self, value_self = rk[:, lanes], rv[:, lanes]
        query = jnp.concatenate([q[:, head_lanes(h, i)] for i in range(GROUP)], 0)
        grad = jnp.concatenate(
            [jnp.where(live, og[:, head_lanes(h, i)], jnp.zeros((), BF16)) for i in range(GROUP)], 0
        )
        both = held[h].reshape(prompt, 2 * HEAD_DIM)
        key, value = both[:, :HEAD_DIM], both[:, HEAD_DIM:]
        masks = jnp.concatenate([bias[...]] * GROUP, 1)
        causals = jnp.concatenate([causal] * GROUP, 1)
        score_p = nt(key, query) + masks
        score_s = nt(key_self, query) + causals
        top = jnp.maximum(
            jnp.max(score_p, 0, keepdims=True), jnp.max(score_s, 0, keepdims=True)
        )
        factor = scaling * math.log2(math.e)
        exp_p = jnp.exp2((score_p - top) * factor)
        exp_s = jnp.exp2((score_s - top) * factor)
        inverse = 1.0 / (jnp.sum(exp_p, 0, keepdims=True) + jnp.sum(exp_s, 0, keepdims=True))
        weight_p, weight_s = exp_p * inverse, exp_s * inverse
        low_p, low_s = weight_p.astype(BF16), weight_s.astype(BF16)
        part_v = nn(low_p, grad)
        gw_p, gw_s = nt(value, grad), nt(value_self, grad)
        dot = jnp.sum(weight_p * gw_p, 0, keepdims=True) + jnp.sum(weight_s * gw_s, 0, keepdims=True)
        sg_p = (weight_p * (gw_p - dot)).astype(BF16)
        sg_s = (weight_s * (gw_s - dot)).astype(BF16)
        part_k = nn(sg_p, query)
        shape = (CORES, PAIRS, far, rows, HEAD_DIM)
        part[h, :, :, :, :, :HEAD_DIM] = part_k.astype(BF16).reshape(shape)
        part[h, :, :, :, :, HEAD_DIM:] = part_v.astype(BF16).reshape(shape)
        reduce_core(h).start()
        between()
        out_t = tn(value, low_p) + tn(value_self, low_s)
        dq_t = (tn(key, sg_p) + tn(key_self, sg_s)) * scaling
        for i in range(GROUP):
            cut = slice(i * length, (i + 1) * length)
            o_ref[0, :, head_lanes(h, i)] = jnp.where(live, out_t[:, cut].T, 0.0).astype(BF16)
            dq_ref[0, :, head_lanes(h, i)] = dq_t[:, cut].T.astype(BF16)
        dk_ref[0, :, lanes] = (nn(sg_s, query) * scaling).astype(BF16)
        dv_ref[0, :, lanes] = nn(low_s, grad).astype(BF16)

    last = KV_HEADS - 1
    pass_pair(0)
    start_far(2)
    pass_pair(1)
    start_far(3)
    pass_core(0)
    for load in loads[2:]:
        load.wait()

    def between(h):
        if h == 0:
            pass_pair(2)
            pass_core(1)
        if h == 1:
            pass_core(2)
        if h >= 1:
            add_pair(h - 1)

    for h in range(KV_HEADS):
        gather_core(h, 1 - c).wait_recv()
        compute(h, functools.partial(between, h))
        if h == 0:
            pass_pair(3)
        if h == 1:
            pass_core(3)
        add_core(h)
    add_far(0)
    add_pair(last)
    for h in range(1, last):
        add_far(h)
    for h in range(KV_HEADS):
        for d in range(1, far):
            gather_far(h, d, z).wait_send()
        for d in range(far):
            gather_pair(h, d, y).wait_send()
            reduce_pair(h, d).wait_send()
        gather_core(h, c).wait_send()
        reduce_core(h).wait_send()
    add_far(last)
    for h in range(KV_HEADS):
        for d in range(1, far):
            reduce_far(h, d).wait_send()


def store_kernel(*refs):
    count = len(refs) // 2
    sems = refs[-1]
    copies = [pltpu.make_async_copy(refs[i], refs[count + i], sems.at[i]) for i in range(count)]
    for copy in copies:
        copy.start()
    for copy in copies:
        copy.wait()


def on_device(far, queries, resp_keys, resp_values, out_grad, resp_lengths, prompt_keys, prompt_values, prompt_length):
    length, width = queries.shape[1:]
    rows, kv_width = prompt_keys.shape
    prompt = rows * far * PAIRS * CORES
    any_spec = pl.BlockSpec(memory_space=pltpu.HBM)
    vmem = pl.BlockSpec(memory_space=pltpu.VMEM)
    smem = pl.BlockSpec(memory_space=pltpu.SMEM)
    both = 2 * HEAD_DIM
    dma = pltpu.SemaphoreType.DMA
    results = pl.pallas_call(
        functools.partial(kernel, far),
        out_shape=(
            pltpu.VMEM(queries.shape, BF16),
            pltpu.VMEM(queries.shape, BF16),
            pltpu.VMEM(resp_keys.shape, BF16),
            pltpu.VMEM(resp_keys.shape, BF16),
            pltpu.VMEM(prompt_keys.shape, F32),
            pltpu.VMEM(prompt_keys.shape, F32),
        ),
        in_specs=[any_spec, any_spec, any_spec, any_spec, smem, any_spec, any_spec, smem],
        out_specs=(vmem,) * 6,
        scratch_shapes=[
            pltpu.VMEM((length, width), BF16),
            pltpu.VMEM((length, width), BF16),
            pltpu.VMEM((length, kv_width), BF16),
            pltpu.VMEM((length, kv_width), BF16),
            pltpu.VMEM((rows, kv_width), BF16),
            pltpu.VMEM((rows, kv_width), BF16),
            pltpu.VMEM((KV_HEADS, CORES, PAIRS, far, rows, both), BF16),
            pltpu.VMEM((KV_HEADS, CORES, PAIRS, far, rows, both), BF16),
            pltpu.VMEM((KV_HEADS, PAIRS, far, rows, both), BF16),
            pltpu.VMEM((KV_HEADS, far, rows, both), BF16),
            pltpu.VMEM((KV_HEADS, far, rows, both), BF16),
            pltpu.VMEM((KV_HEADS, far - 1, rows, both), BF16),
            pltpu.VMEM((KV_HEADS, far - 1, rows, both), BF16),
            pltpu.VMEM((prompt, length), F32),
            dma((6,)),
            dma((KV_HEADS, far - 1)), dma((KV_HEADS, far - 1)),
            dma((KV_HEADS, far)), dma((KV_HEADS, far)),
            dma((KV_HEADS,)), dma((KV_HEADS,)),
            dma((KV_HEADS,)), dma((KV_HEADS,)),
            dma((KV_HEADS, far)), dma((KV_HEADS, far)),
            dma((KV_HEADS, far - 1)), dma((KV_HEADS, far - 1)),
        ],
        compiler_params=pltpu.CompilerParams(
            collective_id=0, has_side_effects=True, vmem_limit_bytes=62 * 1024 * 1024
        ),
    )(queries, resp_keys, resp_values, out_grad, resp_lengths, prompt_keys, prompt_values, prompt_length)
    return pl.pallas_call(
        store_kernel,
        out_shape=tuple(jax.ShapeDtypeStruct(x.shape, x.dtype) for x in results),
        in_specs=[vmem] * 6,
        out_specs=(any_spec,) * 6,
        scratch_shapes=[dma((6,))],
        compiler_params=pltpu.CompilerParams(vmem_limit_bytes=2 * 1024 * 1024),
    )(*results)


def solution(mesh):
    far = mesh.shape["resp"] // (CORES * PAIRS)
    shard = P(("groups", "resp"), None, None)
    flat = P(("groups", "resp"), None)
    return jax.shard_map(
        functools.partial(on_device, far),
        mesh=mesh,
        in_specs=(shard, shard, shard, shard, P(("groups", "resp")), flat, flat, P("groups")),
        out_specs=(shard, shard, shard, shard, flat, flat),
        check_vma=False,
    )
```

```python
import functools
import math

import jax
import jax.numpy as jnp
from jax import lax
from jax.experimental import pallas as pl
from jax.experimental.pallas import tpu as pltpu
from jax.sharding import PartitionSpec as P

HEADS = 16
KV_HEADS = 4
HEAD_DIM = 128
GROUP = HEADS // KV_HEADS
CORES = 2
PAIRS = 2
F32 = jnp.float32
BF16 = jnp.bfloat16


def nt(left, right):
    return lax.dot_general(left, right, (((1,), (1,)), ((), ())), preferred_element_type=F32)


def tn(left, right):
    return lax.dot_general(left, right, (((0,), (0,)), ((), ())), preferred_element_type=F32)


def nn(left, right):
    return lax.dot_general(left, right, (((1,), (0,)), ((), ())), preferred_element_type=F32)


def kernel(
    far,
    q_hbm, rk_hbm, rv_hbm, og_hbm, len_ref, pk_hbm, pv_hbm, plen_ref,
    o_ref, dq_ref, dk_ref, dv_ref, dpk_ref, dpv_ref,
    q, og, rk, rv, pk, pv, held, part, from_core, core_sum, from_pair, pair_sum, from_far, bias,
    load_sem,
    s1, r1, s2, r2, s3, r3, sa, ra, sb, rb, sc, rc,
):
    me = lax.axis_index("resp")
    c = lax.rem(me, CORES)
    y = lax.rem(lax.div(me, CORES), PAIRS)
    z = lax.div(me, CORES * PAIRS)
    rows = pk_hbm.shape[0]
    prompt = rows * far * PAIRS * CORES
    length = q_hbm.shape[1]
    wide = GROUP * length
    scaling = HEAD_DIM ** -0.5

    def device(zz, yy, cc):
        return {"resp": (zz * PAIRS + yy) * CORES + cc}

    def remote(src, dst, send, recv, target):
        return pltpu.make_async_remote_copy(
            src_ref=src, dst_ref=dst, send_sem=send, recv_sem=recv,
            device_id=target, device_id_type=pl.DeviceIdType.MESH,
        )

    def ahead(d):
        return lax.rem(z + d, far)

    def behind(d):
        return lax.rem(z + (far - d), far)

    pair_dev = device(z, 1 - y, c)
    core_dev = device(z, y, 1 - c)

    loads = [
        pltpu.make_async_copy(src, dst, load_sem.at[i])
        for i, (src, dst) in enumerate((
            (pk_hbm, pk), (pv_hbm, pv), (rk_hbm.at[0], rk), (rv_hbm.at[0], rv),
            (q_hbm.at[0], q), (og_hbm.at[0], og),
        ))
    ]
    for load in loads:
        load.start()

    barrier = pltpu.get_barrier_semaphore()
    for d in range(1, far):
        pl.semaphore_signal(barrier, inc=1, device_id=device(ahead(d), y, c),
                            device_id_type=pl.DeviceIdType.MESH)
    pl.semaphore_signal(barrier, inc=1, device_id=pair_dev, device_id_type=pl.DeviceIdType.MESH)
    pl.semaphore_signal(barrier, inc=1, device_id=core_dev, device_id_type=pl.DeviceIdType.MESH)

    loads[0].wait()
    loads[1].wait()
    for h in range(KV_HEADS):
        lanes = slice(h * HEAD_DIM, (h + 1) * HEAD_DIM)
        held[h, c, y, z, :, :HEAD_DIM] = pk[:, lanes]
        held[h, c, y, z, :, HEAD_DIM:] = pv[:, lanes]

    pl.semaphore_wait(barrier, far + 1)

    def gather_far(h, d, slot):
        return remote(held.at[h, c, y, slot], held.at[h, c, y, slot],
                      s1.at[h, d - 1], r1.at[h, d - 1], device(ahead(d), y, c))

    def gather_pair(h, d, yy):
        slot = behind(d)
        return remote(held.at[h, c, yy, slot], held.at[h, c, yy, slot],
                      s2.at[h, d], r2.at[h, d], pair_dev)

    def gather_core(h, cc):
        return remote(held.at[h, cc], held.at[h, cc], s3.at[h], r3.at[h], core_dev)

    def start_far(h):
        for d in range(1, far):
            gather_far(h, d, z).start()
        gather_pair(h, 0, y).start()

    def pass_pair(h):
        for d in range(1, far):
            gather_far(h, d, behind(d)).wait_recv()
            gather_pair(h, d, y).start()

    def pass_core(h):
        for d in range(far):
            gather_pair(h, d, 1 - y).wait_recv()
        gather_core(h, c).start()

    steps = [*range(1, far), 0]

    def reduce_core(h):
        return remote(part.at[h, 1 - c], from_core.at[h], sa.at[h], ra.at[h], core_dev)

    def reduce_pair(h, d):
        slot = ahead(d)
        return remote(core_sum.at[h, slot], from_pair.at[h, slot], sb.at[h, d], rb.at[h, d], pair_dev)

    def reduce_far(h, d):
        return remote(pair_sum.at[h, d - 1], from_far.at[h, d - 1],
                      sc.at[h, d - 1], rc.at[h, d - 1], device(ahead(d), y, c))

    def add_core(h):
        reduce_core(h).wait_recv()
        for d in steps:
            slot = ahead(d)
            core_sum[h, slot] = (
                part[h, c, 1 - y, slot].astype(F32) + from_core[h, 1 - y, slot].astype(F32)
            ).astype(BF16)
            reduce_pair(h, d).start()

    def own_sum(h, d):
        slot = ahead(d)
        reduce_pair(h, d).wait_recv()
        return (
            part[h, c, y, slot].astype(F32)
            + from_core[h, y, slot].astype(F32)
            + from_pair[h, slot].astype(F32)
        )

    def add_pair(h):
        for d in range(1, far):
            pair_sum[h, d - 1] = own_sum(h, d).astype(BF16)
            reduce_far(h, d).start()

    def add_far(h):
        total = own_sum(h, 0)
        for d in range(1, far):
            reduce_far(h, d).wait_recv()
            total = total + from_far[h, d - 1].astype(F32)
        lanes = slice(h * HEAD_DIM, (h + 1) * HEAD_DIM)
        dpk_ref[:, lanes] = total[:, :HEAD_DIM] * scaling
        dpv_ref[:, lanes] = total[:, HEAD_DIM:]

    start_far(0)
    start_far(1)

    index = lax.broadcasted_iota(jnp.int32, (prompt, length), 0)
    block = lax.div(index, rows)
    owner = (
        lax.rem(block, far) * (PAIRS * CORES)
        + lax.rem(lax.div(block, far), PAIRS) * CORES
        + lax.div(block, far * PAIRS)
    )
    position = owner * rows + lax.rem(index, rows)
    bias[...] = jnp.where(position < plen_ref[0], 0.0, -jnp.inf)
    below = lax.broadcasted_iota(jnp.int32, (length, length), 0)
    after = lax.broadcasted_iota(jnp.int32, (length, length), 1)
    causal = jnp.where(below <= after, 0.0, -jnp.inf)
    live = below < len_ref[0]

    def head_lanes(h, i):
        return slice((h * GROUP + i) * HEAD_DIM, (h * GROUP + i + 1) * HEAD_DIM)

    def compute(h, between):
        lanes = slice(h * HEAD_DIM, (h + 1) * HEAD_DIM)
        key_self, value_self = rk[:, lanes], rv[:, lanes]
        query = jnp.concatenate([q[:, head_lanes(h, i)] for i in range(GROUP)], 0)
        grad = jnp.concatenate(
            [jnp.where(live, og[:, head_lanes(h, i)], jnp.zeros((), BF16)) for i in range(GROUP)], 0
        )
        both = held[h].reshape(prompt, 2 * HEAD_DIM)
        key, value = both[:, :HEAD_DIM], both[:, HEAD_DIM:]
        masks = jnp.concatenate([bias[...]] * GROUP, 1)
        causals = jnp.concatenate([causal] * GROUP, 1)
        score_p = nt(key, query) + masks
        score_s = nt(key_self, query) + causals
        top = jnp.maximum(
            jnp.max(score_p, 0, keepdims=True), jnp.max(score_s, 0, keepdims=True)
        )
        factor = scaling * math.log2(math.e)
        exp_p = jnp.exp2((score_p - top) * factor)
        exp_s = jnp.exp2((score_s - top) * factor)
        inverse = 1.0 / (jnp.sum(exp_p, 0, keepdims=True) + jnp.sum(exp_s, 0, keepdims=True))
        weight_p, weight_s = exp_p * inverse, exp_s * inverse
        low_p, low_s = weight_p.astype(BF16), weight_s.astype(BF16)
        part_v = nn(low_p, grad)
        gw_p, gw_s = nt(value, grad), nt(value_self, grad)
        dot = jnp.sum(weight_p * gw_p, 0, keepdims=True) + jnp.sum(weight_s * gw_s, 0, keepdims=True)
        sg_p = (weight_p * (gw_p - dot)).astype(BF16)
        sg_s = (weight_s * (gw_s - dot)).astype(BF16)
        part_k = nn(sg_p, query)
        shape = (CORES, PAIRS, far, rows, HEAD_DIM)
        part[h, :, :, :, :, :HEAD_DIM] = part_k.astype(BF16).reshape(shape)
        part[h, :, :, :, :, HEAD_DIM:] = part_v.astype(BF16).reshape(shape)
        reduce_core(h).start()
        between()
        out_t = tn(value, low_p) + tn(value_self, low_s)
        dq_t = (tn(key, sg_p) + tn(key_self, sg_s)) * scaling
        for i in range(GROUP):
            cut = slice(i * length, (i + 1) * length)
            o_ref[0, :, head_lanes(h, i)] = jnp.where(live, out_t[:, cut].T, 0.0).astype(BF16)
            dq_ref[0, :, head_lanes(h, i)] = dq_t[:, cut].T.astype(BF16)
        dk_ref[0, :, lanes] = (nn(sg_s, query) * scaling).astype(BF16)
        dv_ref[0, :, lanes] = nn(low_s, grad).astype(BF16)

    last = KV_HEADS - 1
    pass_pair(0)
    start_far(2)
    pass_pair(1)
    start_far(3)
    pass_core(0)
    for load in loads[2:]:
        load.wait()

    def between(h):
        if h == 0:
            pass_pair(2)
            pass_core(1)
        if h == 1:
            pass_core(2)
        if h >= 1:
            add_pair(h - 1)
        if h == last:
            add_core(h)

    for h in range(KV_HEADS):
        gather_core(h, 1 - c).wait_recv()
        compute(h, functools.partial(between, h))
        if h == 0:
            pass_pair(3)
        if h == 1:
            pass_core(3)
        if h < last:
            add_core(h)
    add_far(0)
    add_pair(last)
    for h in range(1, last):
        add_far(h)
    for h in range(KV_HEADS):
        for d in range(1, far):
            gather_far(h, d, z).wait_send()
        for d in range(far):
            gather_pair(h, d, y).wait_send()
            reduce_pair(h, d).wait_send()
        gather_core(h, c).wait_send()
        reduce_core(h).wait_send()
    add_far(last)
    for h in range(KV_HEADS):
        for d in range(1, far):
            reduce_far(h, d).wait_send()


def store_kernel(*refs):
    count = len(refs) // 2
    sems = refs[-1]
    copies = [pltpu.make_async_copy(refs[i], refs[count + i], sems.at[i]) for i in range(count)]
    for copy in copies:
        copy.start()
    for copy in copies:
        copy.wait()


def on_device(far, queries, resp_keys, resp_values, out_grad, resp_lengths, prompt_keys, prompt_values, prompt_length):
    length, width = queries.shape[1:]
    rows, kv_width = prompt_keys.shape
    prompt = rows * far * PAIRS * CORES
    any_spec = pl.BlockSpec(memory_space=pltpu.HBM)
    vmem = pl.BlockSpec(memory_space=pltpu.VMEM)
    smem = pl.BlockSpec(memory_space=pltpu.SMEM)
    both = 2 * HEAD_DIM
    dma = pltpu.SemaphoreType.DMA
    results = pl.pallas_call(
        functools.partial(kernel, far),
        out_shape=(
            pltpu.VMEM(queries.shape, BF16),
            pltpu.VMEM(queries.shape, BF16),
            pltpu.VMEM(resp_keys.shape, BF16),
            pltpu.VMEM(resp_keys.shape, BF16),
            pltpu.VMEM(prompt_keys.shape, F32),
            pltpu.VMEM(prompt_keys.shape, F32),
        ),
        in_specs=[any_spec, any_spec, any_spec, any_spec, smem, any_spec, any_spec, smem],
        out_specs=(vmem,) * 6,
        scratch_shapes=[
            pltpu.VMEM((length, width), BF16),
            pltpu.VMEM((length, width), BF16),
            pltpu.VMEM((length, kv_width), BF16),
            pltpu.VMEM((length, kv_width), BF16),
            pltpu.VMEM((rows, kv_width), BF16),
            pltpu.VMEM((rows, kv_width), BF16),
            pltpu.VMEM((KV_HEADS, CORES, PAIRS, far, rows, both), BF16),
            pltpu.VMEM((KV_HEADS, CORES, PAIRS, far, rows, both), BF16),
            pltpu.VMEM((KV_HEADS, PAIRS, far, rows, both), BF16),
            pltpu.VMEM((KV_HEADS, far, rows, both), BF16),
            pltpu.VMEM((KV_HEADS, far, rows, both), BF16),
            pltpu.VMEM((KV_HEADS, far - 1, rows, both), BF16),
            pltpu.VMEM((KV_HEADS, far - 1, rows, both), BF16),
            pltpu.VMEM((prompt, length), F32),
            dma((6,)),
            dma((KV_HEADS, far - 1)), dma((KV_HEADS, far - 1)),
            dma((KV_HEADS, far)), dma((KV_HEADS, far)),
            dma((KV_HEADS,)), dma((KV_HEADS,)),
            dma((KV_HEADS,)), dma((KV_HEADS,)),
            dma((KV_HEADS, far)), dma((KV_HEADS, far)),
            dma((KV_HEADS, far - 1)), dma((KV_HEADS, far - 1)),
        ],
        compiler_params=pltpu.CompilerParams(
            collective_id=0, has_side_effects=True, vmem_limit_bytes=62 * 1024 * 1024
        ),
    )(queries, resp_keys, resp_values, out_grad, resp_lengths, prompt_keys, prompt_values, prompt_length)
    return pl.pallas_call(
        store_kernel,
        out_shape=tuple(jax.ShapeDtypeStruct(x.shape, x.dtype) for x in results),
        in_specs=[vmem] * 6,
        out_specs=(any_spec,) * 6,
        scratch_shapes=[dma((6,))],
        compiler_params=pltpu.CompilerParams(vmem_limit_bytes=2 * 1024 * 1024),
    )(*results)


def solution(mesh):
    far = mesh.shape["resp"] // (CORES * PAIRS)
    shard = P(("groups", "resp"), None, None)
    flat = P(("groups", "resp"), None)
    return jax.shard_map(
        functools.partial(on_device, far),
        mesh=mesh,
        in_specs=(shard, shard, shard, shard, P(("groups", "resp")), flat, flat, P("groups")),
        out_specs=(shard, shard, shard, shard, flat, flat),
        check_vma=False,
    )
```
